32 devices in a mesh: groups: 2 (over x), space: 8 (over z, y), beam: 2 (over core).
Axes of the slice: x: 2, y: 2, z: 4, core: 2. Of those that a mesh axis runs over, the one named last changes fastest.
Arguments:
- s_matrix: bfloat16 [4096, 256, 480], P(('groups', 'beam'), 'space'), parts along dimension 0, may hold values from -6 to 6
- beam_index: int32 [2048, 2], P('beam'), may hold values from -24 to 23, as said below
- beam_amp: float32 [2048], P('beam'), may hold values from 0.5 to 2
- beam_phase: float32 [2048], P('beam'), may hold values from -3.140625 to 3.140625
- positions: int32 [2, 384, 2], replicated, may hold values from 0 to 239
Outputs:
- intensities: float32 [4, 384, 256, 240], P('groups', ('space', 'beam')), parts along dimension 0
The draws below stay inside these ranges and needn't reach their ends.
There are 2 independent parts, one for each index of `groups`. The reference program is written for one: setup_inputs(seed, part) draws one part's arguments, and reference() takes and returns one part's arrays. A program takes and returns all parts, laid end to end along the dimension named above; an argument that names none is the same for every part. Nothing has to cross between parts.
Inputs may be any that keep to these rules, and one draw needn't show every extreme that they name: `beam_index`: no two beams have the same wave-vector.
All inputs are finite; a program needn't handle non-finite values.
Results may differ from the reference program's by a relative error of at most 0.0072.
Values may be sent and summed in bfloat16 or wider, within the bound.
A program may use at most 192 MiB of HBM per device.

```python
import math
import jax
import jax.numpy as jnp
from jax import lax

NB = 2048
RY = 256
RX = 240
NBATCH = 2
P_SIZE = 384
N_BEAM = 2


def draw_beam_index(key, part):
    middle = jax.random.permutation(jax.random.fold_in(key, 11), jnp.arange(1, 2303, dtype=jnp.int32))
    cells = jnp.concatenate([jnp.array([0, 2303], dtype=jnp.int32), middle], 0)[:NB]
    order = jax.random.permutation(jax.random.fold_in(key, 12), jnp.arange(NB, dtype=jnp.int32))
    cells = cells[order]
    row_part = cells // 48 - 24
    col_part = cells % 48 - 24
    return jnp.stack([row_part, col_part], 1).astype(jnp.int32)


def with_ends(values, key, least, top_value):
    place = [jax.random.randint(jax.random.fold_in(key, axis), (), 0, length) for axis, length in enumerate(values.shape)]
    main_axis = values.shape.index(max(values.shape))
    neighbour = place[:main_axis] + [(place[main_axis] + 1) % values.shape[main_axis]] + place[main_axis + 1:]
    return values.at[tuple(place)].set(least).at[tuple(neighbour)].set(top_value)


def shard_levels(rng, extent, shards, smallest, top_value):
    def one(axis_at, blocks):
        heights = jax.random.uniform(jax.random.fold_in(jax.random.fold_in(rng, 6), axis_at), (blocks,), jnp.float32, smallest / len(shards), top_value / len(shards))
        return jnp.repeat(jnp.exp(heights), extent[axis_at] // blocks).reshape((-1,) + (1,) * (len(extent) - axis_at - 1))

    loudness = one(*shards[0])
    for cut in shards[1:]:
        loudness = loudness * one(*cut)
    return loudness


def scatter_about(key, dims, width, bound, shards=(), kind=jnp.bfloat16):
    drawn = jax.random.normal(key, dims, jnp.float32) * width
    if len(shards) > 0:
        drawn = shard_levels(key, dims, shards, -0.22, 0.18) * drawn
    return jnp.clip(drawn, min=-bound, max=bound).astype(kind)


def setup_inputs(seed: int = 0, part: int = 0) -> dict:
    keys = jax.random.split(jax.random.key(seed), 6)
    part_keys = jax.random.split(jax.random.fold_in(keys[5], part), 6)
    return {
        "s_matrix": scatter_about(part_keys[0], (NB, RY, 2 * RX), 1.0, 6.0, ((0, 2), (1, 8))),
        "beam_index": draw_beam_index(jax.random.fold_in(keys[5], 71), part),
        "beam_amp": jnp.clip(jnp.exp(math.log(2.0) - 1.3862944 * jax.random.uniform(keys[2], (NB,), jnp.float32) ** shard_levels(keys[2], (NB,), ((0, 2),), -0.2, 0.2)), 0.5, 2.0),
        "beam_phase": jnp.clip(jax.random.uniform(keys[3], (NB,), jnp.float32, -3.140625, 3.140625), -3.140625, 3.140625),
        "positions": with_ends(jax.random.randint(keys[4], (NBATCH, P_SIZE, 2), 0, RX), jax.random.fold_in(keys[4], 1), 0, RX - 1).astype(jnp.int32),
    }


def dft_tables():
    xs = jnp.arange(RX, dtype=jnp.int32)
    prod_x = jnp.mod(xs[:, None] * xs[None, :], RX).astype(jnp.float32)
    angle_x = 2.0 * math.pi / RX * prod_x
    cos_x = jnp.cos(angle_x) / math.sqrt(RX)
    sin_x = jnp.sin(angle_x) / math.sqrt(RX)
    table_x = jnp.concatenate([jnp.concatenate([cos_x, -sin_x], 1), jnp.concatenate([sin_x, cos_x], 1)], 0).astype(jnp.bfloat16)
    ys = jnp.arange(RY, dtype=jnp.int32)
    prod_y = jnp.mod(ys[:, None] * ys[None, :], RY).astype(jnp.float32)
    angle_y = 2.0 * math.pi / RY * prod_y
    table_y = jnp.concatenate([jnp.cos(angle_y), jnp.sin(angle_y)], 0) / math.sqrt(RY)
    return (table_x, table_y.astype(jnp.bfloat16))

def coefficients(spots, beam_index, beam_amp, beam_phase):
    rows_part = jnp.mod(spots[:, 0:1] * beam_index[None, :, 0], RY).astype(jnp.float32)
    cols_part = jnp.mod(spots[:, 1:2] * beam_index[None, :, 1], RX).astype(jnp.float32)
    theta = beam_phase[None, :] - 2.0 * math.pi * (rows_part / RY + cols_part / RX)
    scale = beam_amp[None, :] / math.sqrt(NB)
    return ((scale * jnp.cos(theta)).astype(jnp.bfloat16), (scale * jnp.sin(theta)).astype(jnp.bfloat16))

def reference(s_matrix, beam_index, beam_amp, beam_phase, positions):
    table_x, table_y = dft_tables()
    block = NB // N_BEAM
    results = []
    for batch in range(NBATCH):
        coef_re, coef_im = coefficients(positions[batch], beam_index, beam_amp, beam_phase)
        total = jnp.zeros((P_SIZE, RY, 2 * RX), jnp.float32)
        for part in range(N_BEAM):
            flat = s_matrix[part * block:(part + 1) * block].reshape(block, RY * 2 * RX)
            real_side = jnp.dot(coef_re[:, part * block:(part + 1) * block], flat, preferred_element_type=jnp.float32).reshape(P_SIZE, RY, 2 * RX)
            imag_side = jnp.dot(coef_im[:, part * block:(part + 1) * block], flat, preferred_element_type=jnp.float32).reshape(P_SIZE, RY, 2 * RX)
            wave_re = real_side[..., :RX] - imag_side[..., RX:]
            wave_im = real_side[..., RX:] + imag_side[..., :RX]
            rounded = lax.optimization_barrier(jnp.concatenate([wave_re, wave_im], -1).astype(jnp.bfloat16))
            total = total + rounded.astype(jnp.float32)
        wave = total.astype(jnp.bfloat16)
        half = jnp.dot(wave.reshape(P_SIZE * RY, 2 * RX), table_x, preferred_element_type=jnp.float32)
        half = half.astype(jnp.bfloat16).reshape(P_SIZE, RY, 2 * RX)
        spectrum = jnp.einsum('vy,pyc->pvc', table_y.astype(jnp.float32), half.astype(jnp.float32))
        spec_re = spectrum[:, :RY, :RX] + spectrum[:, RY:, RX:]
        spec_im = spectrum[:, :RY, RX:] - spectrum[:, RY:, :RX]
        results.append(spec_re * spec_re + spec_im * spec_im)
    return jnp.stack(results, 0)
```

```python
import functools
import math

import jax
import jax.numpy as jnp
from jax import lax
from jax.experimental import pallas as pl
from jax.experimental.pallas import tpu as pltpu
from jax.sharding import PartitionSpec as P

VMEM = 56 * 1024 * 1024


def dft_tables(rows, cols, n_space, pack):
    xs = jnp.arange(cols, dtype=jnp.int32)
    prod_x = jnp.mod(xs[:, None] * xs[None, :], cols).astype(jnp.float32)
    angle_x = 2.0 * math.pi / cols * prod_x
    cos_x = jnp.cos(angle_x) / math.sqrt(cols)
    sin_x = jnp.sin(angle_x) / math.sqrt(cols)
    table_x = jnp.concatenate(
        [jnp.concatenate([cos_x, -sin_x], 1), jnp.concatenate([sin_x, cos_x], 1)], 0
    ).astype(jnp.bfloat16)
    ys = jnp.arange(rows, dtype=jnp.int32)
    order = ys.reshape(n_space, pack, -1).transpose(1, 0, 2).reshape(-1)
    prod_y = jnp.mod(order[:, None] * ys[None, :], rows).astype(jnp.float32)
    angle_y = 2.0 * math.pi / rows * prod_y
    table_y = jnp.concatenate([jnp.cos(angle_y), jnp.sin(angle_y)], 1) / math.sqrt(rows)
    return table_x, table_y.astype(jnp.bfloat16)


def coefficients(spots, beam_index, beam_amp, beam_phase, rows, cols, n_beams):
    rows_part = jnp.mod(spots[:, 0:1] * beam_index[None, :, 0], rows).astype(jnp.float32)
    cols_part = jnp.mod(spots[:, 1:2] * beam_index[None, :, 1], cols).astype(jnp.float32)
    theta = beam_phase[None, :] - 2.0 * math.pi * (rows_part / rows + cols_part / cols)
    scale = beam_amp[None, :] / math.sqrt(n_beams)
    return jnp.concatenate(
        [(scale * jnp.cos(theta)).astype(jnp.bfloat16), (scale * jnp.sin(theta)).astype(jnp.bfloat16)], 0
    )


def gemm_kernel(c_ref, s_ref, o_ref):
    n_rows, width, _ = s_ref.shape
    cols = width // 2
    n_beam, _, per, _ = o_ref.shape
    probes = n_beam * per
    dims = (((1,), (1,)), ((), ()))
    for y in range(n_rows):
        on_re = lax.dot_general(c_ref[...], s_ref[y, :cols, :], dims, preferred_element_type=jnp.float32)
        on_im = lax.dot_general(c_ref[...], s_ref[y, cols:, :], dims, preferred_element_type=jnp.float32)
        wave_re = (on_re[:probes] - on_im[probes:]).astype(jnp.bfloat16)
        wave_im = (on_im[:probes] + on_re[probes:]).astype(jnp.bfloat16)
        for h in range(n_beam):
            o_ref[h, y, :, :cols] = wave_re[h * per:(h + 1) * per]
            o_ref[h, y, :, cols:] = wave_im[h * per:(h + 1) * per]


def waves(coef, s_rows, n_beam):
    local_rows, width, beams = s_rows.shape
    probes = coef.shape[0] // 2
    block = 4
    return pl.pallas_call(
        gemm_kernel,
        grid=(local_rows // block,),
        in_specs=[
            pl.BlockSpec((2 * probes, beams), lambda i: (0, 0)),
            pl.BlockSpec((block, width, beams), lambda i: (i, 0, 0)),
        ],
        out_specs=pl.BlockSpec((n_beam, block, probes // n_beam, width), lambda i: (0, i, 0, 0)),
        out_shape=jax.ShapeDtypeStruct((n_beam, local_rows, probes // n_beam, width), jnp.bfloat16),
        compiler_params=pltpu.CompilerParams(vmem_limit_bytes=VMEM),
        cost_estimate=pl.CostEstimate(
            flops=4 * probes * beams * local_rows * width,
            bytes_accessed=2 * local_rows * width * beams,
            transcendentals=0,
        ),
        name="waves",
    )(coef, s_rows)


def half_kernel(pack, w_ref, t_ref, o_ref):
    local_rows, per, width = w_ref.shape
    half = jnp.dot(w_ref[...].reshape(local_rows * per, width), t_ref[...], preferred_element_type=jnp.float32)
    half = jnp.swapaxes(half.reshape(local_rows, per, width), 0, 1)
    part = local_rows // pack
    for q in range(pack):
        o_ref[:, :, q * width:(q + 1) * width] = half[:, q * part:(q + 1) * part, :].astype(jnp.bfloat16)


def halves(wave, table_x, pack):
    local_rows, per, width = wave.shape
    return pl.pallas_call(
        functools.partial(half_kernel, pack),
        out_shape=jax.ShapeDtypeStruct((per, local_rows // pack, pack * width), jnp.bfloat16),
        compiler_params=pltpu.CompilerParams(vmem_limit_bytes=VMEM),
        cost_estimate=pl.CostEstimate(
            flops=2 * per * local_rows * width * width,
            bytes_accessed=4 * per * local_rows * width,
            transcendentals=0,
        ),
        name="halves",
    )(wave, table_x)


def spectrum_kernel(pack, h_ref, t_ref, *rest):
    o_ref = rest[-1]
    n_space, _, part, packed = h_ref.shape
    width = packed // pack
    cols = width // 2
    rows = n_space * part * pack
    block = h_ref[:, 0].reshape(n_space * part, packed)
    half = jnp.concatenate([block[:, q * width:(q + 1) * width] for q in range(pack)], 0)
    both = lax.dot_general(half, t_ref[...], (((0,), (0,)), ((), ())), preferred_element_type=jnp.float32)
    spec_re = both[:cols, :rows] + both[cols:, rows:]
    spec_im = both[cols:, :rows] - both[:cols, rows:]
    o_ref[0] = spec_re * spec_re + spec_im * spec_im


def spectra(half, table_y, out, first, total, pack):
    n_space, count, part, packed = half.shape
    rows = n_space * part * pack
    cols = packed // pack // 2
    operands = [half, table_y]
    in_specs = [
        pl.BlockSpec((n_space, 1, part, packed), lambda i: (0, i, 0, 0)),
        pl.BlockSpec((rows, 2 * rows), lambda i: (0, 0)),
    ]
    if out is not None:
        operands.append(out)
        in_specs.append(pl.BlockSpec(memory_space=pl.ANY))
    return pl.pallas_call(
        functools.partial(spectrum_kernel, pack),
        grid=(count,),
        in_specs=in_specs,
        out_specs=pl.BlockSpec((1, cols, rows), lambda i: (first + i, 0, 0)),
        out_shape=jax.ShapeDtypeStruct((total, cols, rows), jnp.float32),
        input_output_aliases={} if out is None else {2: 0},
        compiler_params=pltpu.CompilerParams(vmem_limit_bytes=VMEM),
        cost_estimate=pl.CostEstimate(
            flops=8 * count * cols * rows * rows,
            bytes_accessed=8 * count * cols * rows,
            transcendentals=0,
        ),
        name="spectra",
    )(*operands)


def body(s_matrix, beam_index, beam_amp, beam_phase, positions):
    n_space = lax.axis_size("space")
    n_beam = lax.axis_size("beam")
    local_beams, local_rows, width = s_matrix.shape
    cols = width // 2
    rows = local_rows * n_space
    n_batch = positions.shape[0]
    per_device = positions.shape[1] // (n_space * n_beam)
    pack = 4 if local_rows % 32 == 0 else 1
    n_chunk = 3
    count = per_device // n_chunk
    s_rows = jnp.transpose(s_matrix, (1, 2, 0))
    table_x, table_y = dft_tables(rows, cols, n_space, pack)
    blocks = positions.reshape(n_batch, n_space, n_beam, n_chunk, count, 2)
    blocks = jnp.transpose(blocks, (0, 3, 2, 1, 4, 5)).reshape(n_batch * n_chunk, -1, 2)

    out = None
    for chunk in range(n_batch * n_chunk):
        coef = coefficients(
            blocks[chunk], beam_index, beam_amp, beam_phase, rows, cols, local_beams * n_beam
        )
        partial = waves(coef, s_rows, n_beam)
        wave = lax.psum_scatter(partial, "beam", scatter_dimension=0, tiled=True)[0]
        half = halves(wave, table_x, pack)
        half = lax.all_to_all(half, "space", split_axis=0, concat_axis=0, tiled=True)
        half = half.reshape(n_space, count, local_rows // pack, pack * width)
        out = spectra(half, table_y, out, chunk * count, n_batch * per_device, pack)
    out = out.reshape(n_batch, per_device, cols, rows)
    return jnp.swapaxes(out, 2, 3)


def solution(mesh):
    in_specs = (P(("groups", "beam"), "space", None), P("beam", None), P("beam"), P("beam"), P())
    out_specs = P("groups", ("space", "beam"), None, None)
    return jax.shard_map(body, mesh=mesh, in_specs=in_specs, out_specs=out_specs, check_vma=False)
```
